32 devices in a mesh: shard: 2 (over x), tm: 16 (over z, y, core).
Axes of the slice: x: 2, y: 2, z: 4, core: 2. Of those that a mesh axis runs over, the one named last changes fastest.
Arguments:
- latents: bfloat16 [128, 32, 1536], P(('shard', 'tm')), parts along dimension 0, as said below
- w_query: bfloat16 [1536, 1536], replicated, may hold values from -0.15625 to 0.15625
- w_key: bfloat16 [1536, 1536], replicated, may hold values from -0.15625 to 0.15625
- w_value: bfloat16 [1536, 1536], replicated, may hold values from -0.15625 to 0.15625
- w_out: bfloat16 [1536, 1536], replicated, may hold values from -0.15625 to 0.15625
- cotangent: bfloat16 [128, 32, 1536], P(('shard', 'tm')), parts along dimension 0, may hold values from -6 to 6
- memory_ids: int32 [128, 4], P(('shard', 'tm')), parts along dimension 0, may hold values from 0 to 63, as said below
- memory_count: int32 [128], P(('shard', 'tm')), parts along dimension 0, may hold values from 1 to 4
- tile_mask: int32 [128, 2], P(('shard', 'tm')), parts along dimension 0, may hold values 0 or 1
Outputs:
- layer_out: bfloat16 [128, 32, 1536], P(('shard', 'tm')), parts along dimension 0
- latent_grad: bfloat16 [128, 32, 1536], P(('shard', 'tm')), parts along dimension 0
The draws below stay inside these ranges and needn't reach their ends.
There are 2 independent parts, one for each index of `shard`. The reference program is written for one: setup_inputs(seed, part) draws one part's arguments, and reference() takes and returns one part's arrays. A program takes and returns all parts, laid end to end along the dimension named above; an argument that names none is the same for every part. Nothing has to cross between parts.
Inputs may be any that keep to these rules, and one draw needn't show every extreme that they name: `memory_ids`: the 16 entries of the frames of one aligned block of 4 frames (frames b * 4 to b * 4 + 3) lie in 16 different such blocks. `latents`: entries lie between -40 and 40.
All inputs are finite; a program needn't handle non-finite values. No bound on the sum of `tile_mask` on one device may be relied on, other than what follows from the above.
Results may differ from the reference program's by a relative error of at most 0.014.
The reference program's roundings to bfloat16 on the way (of `prob_low`, `mixed`, `out_grad`, `score_grad` and `query_grad`) count: a program that leaves them out, or rounds other values in their place, can miss the bound.
Values may be sent and summed in bfloat16 or wider, within the bound.
A program may use at most 192 MiB of HBM per device.

```python
import math
import jax
import jax.numpy as jnp
from jax import lax

D = 1536
HEADS = 24
TILE = 32
F_DEV = 4
MEM = 4
FRAMES = 64
INNER = 1536


def draw_latents(key, part):
    first_key = jax.random.fold_in(key, 11)
    second_key = jax.random.fold_in(key, 12)
    normal_part = jax.random.truncated_normal(first_key, -4.0, 4.0, (FRAMES, TILE, D), jnp.float32)
    low_log, high_log = (math.log(0.5), math.log(2.0))
    row_scale = jnp.exp(jax.random.uniform(second_key, (FRAMES, TILE, 1), jnp.float32, low_log, high_log))
    return (normal_part * row_scale).astype(jnp.bfloat16)


def draw_memory_ids(key, part):
    block_total = FRAMES // F_DEV

    def one_block(block_index):
        sub_key = jax.random.fold_in(jax.random.fold_in(key, 21), block_index)
        order = jax.random.permutation(jax.random.fold_in(sub_key, 1), block_total)[:F_DEV * MEM]
        offset = jax.random.randint(jax.random.fold_in(sub_key, 2), (F_DEV * MEM,), 0, F_DEV)
        return (order * F_DEV + offset).reshape(F_DEV, MEM)
    chosen = jax.vmap(one_block)(jnp.arange(block_total))
    return chosen.reshape(FRAMES, MEM).astype(jnp.int32)


def place_ends(array, stream_key, smallest, top_value):
    spot = [jax.random.randint(jax.random.fold_in(stream_key, axis), (), 0, length) for axis, length in enumerate(array.shape)]
    longest = array.shape.index(max(array.shape))
    beside = spot[:longest] + [(spot[longest] + 1) % array.shape[longest]] + spot[longest + 1:]
    return array.at[tuple(spot)].set(smallest).at[tuple(beside)].set(top_value)


def block_levels(rng, dims, split, least, high):
    def one(dim, blocks):
        heights = jax.random.uniform(jax.random.fold_in(jax.random.fold_in(rng, 6), dim), (blocks,), jnp.float32, least / len(split), high / len(split))
        return jnp.repeat(jnp.exp(heights), dims[dim] // blocks).reshape((-1,) + (1,) * (len(dims) - dim - 1))

    level = one(*split[0])
    for cut in split[1:]:
        level = level * one(*cut)
    return level


def normal_values(stream_key, dims, scale, bound, cuts=(), held_as=jnp.bfloat16):
    loudness = block_levels(stream_key, dims, cuts, -0.22, 0.18) if cuts else 1.0
    entries = jax.random.normal(stream_key, dims, jnp.float32) * scale * loudness
    return jnp.minimum(jnp.maximum(entries, -bound), bound).astype(held_as)


def setup_inputs(seed: int = 0, part: int = 0) -> dict:
    key_of = jax.random.split(jax.random.key(seed), 10)
    part_splits = jax.random.split(jax.random.fold_in(key_of[9], part), 10)
    latents = draw_latents(jax.random.fold_in(jax.random.fold_in(key_of[9], part), 71), part)
    w_query = normal_values(key_of[1], (D, INNER), D ** -0.5, 0.15625)
    w_key = normal_values(key_of[2], (D, INNER), D ** -0.5, 0.15625)
    w_value = normal_values(key_of[3], (D, INNER), D ** -0.5, 0.15625)
    w_out = normal_values(key_of[4], (INNER, D), INNER ** -0.5, 0.15625)
    cotangent = normal_values(part_splits[5], (FRAMES, TILE, D), 1.0, 6.0, ((0, 16),))
    memory_ids = draw_memory_ids(jax.random.fold_in(jax.random.fold_in(key_of[9], part), 71), part)
    memory_count = place_ends(jax.random.randint(part_splits[7], (FRAMES,), 1, MEM + 1), jax.random.fold_in(part_splits[7], 1), 1, MEM).astype(jnp.int32)
    tile_mask = place_ends((jax.random.randint(part_splits[8], (FRAMES, 2), 0, 4) < 3).astype(jnp.int32), jax.random.fold_in(part_splits[8], 1), 0, 1)
    return {"latents": latents, "w_query": w_query, "w_key": w_key, "w_value": w_value, "w_out": w_out, "cotangent": cotangent, "memory_ids": memory_ids, "memory_count": memory_count, "tile_mask": tile_mask}


def attend_forward(queries, keys, values, valid_mask):
    batch, tile_len, inner_width = queries.shape
    blocks = keys.shape[1]
    head_dim = inner_width // HEADS
    inv_root = 1.0 / math.sqrt(head_dim)
    query_four = queries.astype(jnp.float32).reshape(batch, tile_len, HEADS, head_dim)
    key_four = keys.astype(jnp.float32).reshape(batch, blocks * tile_len, HEADS, head_dim)
    value_four = values.astype(jnp.float32).reshape(batch, blocks * tile_len, HEADS, head_dim)
    scores = jnp.einsum('bqhd,bkhd->bhqk', query_four, key_four) * inv_root
    key_mask = jnp.repeat(valid_mask, tile_len, axis=1) > 0.5
    scores = jnp.where(key_mask[:, None, None, :], scores, -1e+30)
    row_max = lax.optimization_barrier(jnp.max(scores, axis=-1, keepdims=True))
    expo = jnp.exp(scores - row_max)
    attn_prob = expo / lax.optimization_barrier(jnp.sum(expo, axis=-1, keepdims=True))
    prob_low = attn_prob.astype(jnp.bfloat16)
    mixed = jnp.einsum('bhqk,bkhd->bqhd', prob_low.astype(jnp.float32), value_four)
    mixed = mixed.astype(jnp.bfloat16).reshape(batch, tile_len, inner_width)
    return (mixed, attn_prob, prob_low)

def attend_backward(queries, keys, values, attn_prob, prob_low, grad_out):
    batch, tile_len, inner_width = queries.shape
    blocks = keys.shape[1]
    head_dim = inner_width // HEADS
    inv_root = 1.0 / math.sqrt(head_dim)
    query_four = queries.astype(jnp.float32).reshape(batch, tile_len, HEADS, head_dim)
    key_four = keys.astype(jnp.float32).reshape(batch, blocks * tile_len, HEADS, head_dim)
    value_four = values.astype(jnp.float32).reshape(batch, blocks * tile_len, HEADS, head_dim)
    grad_four = grad_out.astype(jnp.float32).reshape(batch, tile_len, HEADS, head_dim)
    prob_grad = jnp.einsum('bqhd,bkhd->bhqk', grad_four, value_four)
    row_delta = lax.optimization_barrier(jnp.sum(attn_prob * prob_grad, axis=-1, keepdims=True))
    score_grad = (attn_prob * (prob_grad - row_delta) * inv_root).astype(jnp.bfloat16)
    query_grad = jnp.einsum('bhqk,bkhd->bqhd', score_grad.astype(jnp.float32), key_four)
    query_grad = query_grad.astype(jnp.bfloat16).reshape(batch, tile_len, inner_width)
    key_grad = jnp.einsum('bhqk,bqhd->bkhd', score_grad.astype(jnp.float32), query_four)
    key_grad = key_grad.astype(jnp.bfloat16).reshape(batch, blocks, tile_len, inner_width)
    value_grad = jnp.einsum('bhqk,bqhd->bkhd', prob_low.astype(jnp.float32), grad_four)
    value_grad = value_grad.astype(jnp.bfloat16).reshape(batch, blocks, tile_len, inner_width)
    return (query_grad, key_grad, value_grad)

def reference(latents, w_query, w_key, w_value, w_out, cotangent, memory_ids, memory_count, tile_mask):
    frames, tile_len, width = latents.shape
    flat_rows = latents.reshape(-1, width)

    def project(weight):
        return jnp.dot(flat_rows, weight, preferred_element_type=jnp.float32).astype(jnp.bfloat16).reshape(frames, tile_len, -1)
    queries = project(w_query)
    keys = project(w_key)
    values = project(w_value)
    inner_width = queries.shape[-1]
    out_grad = jnp.dot(cotangent.reshape(-1, width), w_out.T, preferred_element_type=jnp.float32)
    out_grad = out_grad.astype(jnp.bfloat16).reshape(frames, tile_len, inner_width)

    def frame_step(carry, index):
        key_acc, value_acc = carry
        neighbours = jnp.stack([index, index - 1, index + 1]).astype(jnp.int32)
        block_ids = jnp.concatenate([neighbours, memory_ids[index].astype(jnp.int32)])
        clipped = jnp.clip(block_ids, 0, frames - 1).astype(jnp.int32)
        lower = (tile_mask[index, 0] * (index >= 1)).astype(jnp.float32)
        upper = (tile_mask[index, 1] * (index < frames - 1)).astype(jnp.float32)
        remembered = (jnp.arange(MEM) < memory_count[index]).astype(jnp.float32)
        valid_mask = jnp.concatenate([jnp.ones((1,), jnp.float32), lower[None], upper[None], remembered])
        key_blocks = keys[clipped]
        value_blocks = values[clipped]
        mixed, attn_prob, prob_low = attend_forward(queries[index][None], key_blocks[None], value_blocks[None], valid_mask[None])
        query_grad, key_grad, value_grad = attend_backward(queries[index][None], key_blocks[None], value_blocks[None], attn_prob, prob_low, out_grad[index][None])
        key_acc = key_acc.at[clipped].add(key_grad[0].astype(jnp.float32) * valid_mask[:, None, None])
        value_acc = value_acc.at[clipped].add(value_grad[0].astype(jnp.float32) * valid_mask[:, None, None])
        return ((key_acc, value_acc), (mixed[0], query_grad[0]))
    zeros_acc = jnp.zeros((frames, tile_len, inner_width), jnp.float32)
    (key_acc, value_acc), (mixed, query_grad) = lax.scan(frame_step, (zeros_acc, zeros_acc), jnp.arange(frames, dtype=jnp.int32))
    layer_out = jnp.dot(mixed.reshape(-1, inner_width), w_out, preferred_element_type=jnp.float32)
    layer_out = layer_out.astype(jnp.bfloat16).reshape(frames, tile_len, width)
    key_sum = key_acc.astype(jnp.bfloat16).reshape(-1, inner_width)
    value_sum = value_acc.astype(jnp.bfloat16).reshape(-1, inner_width)
    total = jnp.dot(query_grad.reshape(-1, inner_width), w_query.T, preferred_element_type=jnp.float32)
    total = total + jnp.dot(key_sum, w_key.T, preferred_element_type=jnp.float32)
    total = total + jnp.dot(value_sum, w_value.T, preferred_element_type=jnp.float32)
    return (layer_out, total.astype(jnp.bfloat16).reshape(frames, tile_len, width))
```

```python
import functools
import math

import jax
import jax.numpy as jnp
from jax import lax
from jax.experimental import pallas as pl
from jax.experimental.pallas import tpu as pltpu
from jax.sharding import PartitionSpec as P

HEADS = 24
GROUP = 4
NT = (((1,), (1,)), ((), ()))
NN = (((1,), (0,)), ((), ()))
TN = (((0,), (0,)), ((), ()))


def dot(a, b, dims):
    return lax.dot_general(a, b, dims, preferred_element_type=jnp.float32)


def attend_kernel(
    owners, valid, q_ref, g_ref, k_ext, v_ext, k_mem, v_mem,
    mixed_ref, dq_ref, sums_ref, edge_ref, slots_ref,
    *, frames, mem, tile, head_dim, spare,
):
    width = q_ref.shape[1]
    rows = GROUP * tile
    inv_root = 1.0 / math.sqrt(head_dim)
    own_head = (
        lax.broadcasted_iota(jnp.int32, (rows, width), 0) // tile
        == lax.broadcasted_iota(jnp.int32, (rows, width), 1) // head_dim
    )

    def spread(block):
        tall = jnp.concatenate([block] * GROUP, axis=0)
        return jnp.where(own_head, tall, jnp.zeros_like(tall))

    def fold(tall):
        tall = jnp.where(own_head, tall, 0.0)
        total = tall[0:tile]
        for part in range(1, GROUP):
            total = total + tall[part * tile : (part + 1) * tile]
        return total

    if spare:
        slots_ref[...] = jnp.zeros_like(slots_ref)
    for f in range(frames):
        here = slice(f * tile, (f + 1) * tile)
        near = slice(f * tile, (f + 3) * tile)
        spots = [owners[f * mem + j] for j in range(mem)]

        def gather(ext, far):
            return jnp.concatenate([ext[near, :]] + [far[s] for s in spots], axis=0)

        keys = gather(k_ext, k_mem)
        values = gather(v_ext, v_mem)
        queries = spread(q_ref[here, :])
        grads = spread(g_ref[here, :])
        scores = dot(queries, keys, NT) * inv_root
        scores = jnp.where(valid[f : f + 1, :] > 0.5, scores, -1e30)
        expo = jnp.exp(scores - jnp.max(scores, axis=-1, keepdims=True))
        prob = expo / jnp.sum(expo, axis=-1, keepdims=True)
        low = prob.astype(jnp.bfloat16)
        mixed_ref[here, :] = fold(dot(low, values, NN)).astype(jnp.bfloat16)
        prob_grad = dot(grads, values, NT)
        delta = jnp.sum(prob * prob_grad, axis=-1, keepdims=True)
        score_grad = (prob * (prob_grad - delta) * inv_root).astype(jnp.bfloat16)
        dq_ref[here, :] = fold(dot(score_grad, keys, NN)).astype(jnp.bfloat16)
        parts = (
            dot(score_grad, queries, TN).astype(jnp.bfloat16),
            dot(low, grads, TN).astype(jnp.bfloat16),
        )
        for kv, part in enumerate(parts):
            before = part[0:tile]
            own = part[tile : 2 * tile].astype(jnp.float32)
            after = part[2 * tile : 3 * tile]
            if f == 0:
                edge_ref[0, kv] = before
                sums_ref[kv, here, :] = own
            else:
                back = slice((f - 1) * tile, f * tile)
                sums_ref[kv, back, :] += before.astype(jnp.float32)
                sums_ref[kv, here, :] += own
            if f == frames - 1:
                edge_ref[1, kv] = after
            else:
                sums_ref[kv, (f + 1) * tile : (f + 2) * tile, :] = after.astype(jnp.float32)
            for j in range(mem):
                slots_ref[spots[j], kv] = part[(3 + j) * tile : (4 + j) * tile]


def finish_kernel(
    asked, dq_ref, sums_ref, below_ref, above_ref, back_ref, wq_ref, wk_ref, wv_ref,
    out_ref, acc, total, *, frames, tile,
):
    step = pl.program_id(0)
    acc[...] = sums_ref[...]
    last = slice((frames - 1) * tile, frames * tile)
    for kv in range(2):
        acc[kv, 0:tile, :] += below_ref[kv].astype(jnp.float32)
        acc[kv, last, :] += above_ref[kv].astype(jnp.float32)

    @pl.loop(0, back_ref.shape[0])
    def _(n):
        @pl.when(asked[n] >= 0)
        def _():
            spot = pl.ds(pl.multiple_of(asked[n] * tile, tile), tile)
            for kv in range(2):
                acc[kv, spot, :] += back_ref[n, kv].astype(jnp.float32)

    @pl.when(step == 0)
    def _():
        total[...] = jnp.zeros_like(total)

    total[...] += (
        dot(dq_ref[...], wq_ref[...], NT)
        + dot(acc[0].astype(jnp.bfloat16), wk_ref[...], NT)
        + dot(acc[1].astype(jnp.bfloat16), wv_ref[...], NT)
    )

    @pl.when(step == pl.num_programs(0) - 1)
    def _():
        out_ref[...] = total[...].astype(jnp.bfloat16)


def on_device(
    latents, w_query, w_key, w_value, w_out, cotangent, memory_ids, memory_count, tile_mask
):
    frames, tile, width = latents.shape
    count = lax.axis_size("tm")
    me = lax.axis_index("tm")
    rows = latents.reshape(-1, width)
    mem = memory_ids.shape[1]
    inner = w_query.shape[1]
    head_dim = inner // HEADS
    cols = GROUP * head_dim
    steps = inner // cols
    up = [(i, i + 1) for i in range(count - 1)]
    down = [(i + 1, i) for i in range(count - 1)]

    owners = (memory_ids // frames).reshape(-1).astype(jnp.int32)
    local = (memory_ids % frames).reshape(-1).astype(jnp.int32)
    peers = jnp.arange(count, dtype=jnp.int32)
    matched = owners[None, :] == peers[:, None]
    wanted = jnp.where(
        jnp.any(matched, axis=1), jnp.sum(jnp.where(matched, local[None, :], 0), axis=1), -1
    )
    asked = lax.all_to_all(wanted[:, None], "tm", split_axis=0, concat_axis=0, tiled=True)[:, 0]
    frame_ids = jnp.arange(frames, dtype=jnp.int32)
    selector = (asked[:, None] == frame_ids[None, :]).astype(jnp.bfloat16)
    outgoing = jnp.einsum(
        "nf,ftc->ntc", selector, latents, preferred_element_type=jnp.float32
    ).astype(jnp.bfloat16)
    received = lax.all_to_all(outgoing, "tm", split_axis=0, concat_axis=0, tiled=True)
    below_rows = lax.ppermute(latents[frames - 1], "tm", up)
    above_rows = lax.ppermute(latents[0], "tm", down)

    def project(block, weight):
        return jnp.dot(block, weight, preferred_element_type=jnp.float32).astype(jnp.bfloat16)

    ext_rows = jnp.concatenate([below_rows, rows, above_rows], axis=0)
    queries = project(rows, w_query)
    k_ext = project(ext_rows, w_key)
    v_ext = project(ext_rows, w_value)
    out_grad = lax.dot_general(
        cotangent.reshape(-1, width), w_out, NT, preferred_element_type=jnp.float32
    ).astype(jnp.bfloat16)
    far_rows = received.reshape(count * tile, width)
    k_mem = project(far_rows, w_key).reshape(count, tile, inner)
    v_mem = project(far_rows, w_value).reshape(count, tile, inner)

    global_ids = me * frames + frame_ids
    lower = (tile_mask[:, 0] * (global_ids >= 1)).astype(jnp.float32)
    upper = (tile_mask[:, 1] * (global_ids < frames * count - 1)).astype(jnp.float32)
    kept = (jnp.arange(mem, dtype=jnp.int32)[None, :] < memory_count[:, None]).astype(jnp.float32)
    valid = jnp.concatenate(
        [lower[:, None], jnp.ones((frames, 1), jnp.float32), upper[:, None], kept], axis=1
    )
    valid = jnp.repeat(valid, tile, axis=1)

    own = frames * tile
    flat = lambda n: pl.BlockSpec((n, cols), lambda g, *_: (0, g))
    deep = lambda n: pl.BlockSpec((n, tile, cols), lambda g, *_: (0, 0, g))
    mixed, query_grad, sums, edges, slots = pl.pallas_call(
        functools.partial(
            attend_kernel, frames=frames, mem=mem, tile=tile, head_dim=head_dim,
            spare=count > frames * mem,
        ),
        grid_spec=pltpu.PrefetchScalarGridSpec(
            num_scalar_prefetch=1,
            grid=(steps,),
            in_specs=[
                pl.BlockSpec(valid.shape, lambda g, *_: (0, 0)),
                flat(own), flat(own), flat(own + 2 * tile), flat(own + 2 * tile),
                deep(count), deep(count),
            ],
            out_specs=[
                flat(own), flat(own),
                pl.BlockSpec((2, own, cols), lambda g, *_: (0, 0, g)),
                pl.BlockSpec((2, 2, tile, cols), lambda g, *_: (0, 0, 0, g)),
                pl.BlockSpec((count, 2, tile, cols), lambda g, *_: (0, 0, 0, g)),
            ],
        ),
        out_shape=[
            jax.ShapeDtypeStruct((own, inner), jnp.bfloat16),
            jax.ShapeDtypeStruct((own, inner), jnp.bfloat16),
            jax.ShapeDtypeStruct((2, own, inner), jnp.float32),
            jax.ShapeDtypeStruct((2, 2, tile, inner), jnp.bfloat16),
            jax.ShapeDtypeStruct((count, 2, tile, inner), jnp.bfloat16),
        ],
        compiler_params=pltpu.CompilerParams(vmem_limit_bytes=40 * 2**20),
    )(owners, valid, queries, out_grad, k_ext, v_ext, k_mem, v_mem)

    from_below = lax.ppermute(edges[1], "tm", up)
    from_above = lax.ppermute(edges[0], "tm", down)
    back = lax.all_to_all(slots, "tm", split_axis=0, concat_axis=0, tiled=True)
    layer_out = project(mixed, w_out).reshape(frames, tile, width)
    weight = pl.BlockSpec((width, cols), lambda g, *_: (0, g))
    side = pl.BlockSpec((2, tile, cols), lambda g, *_: (0, 0, g))
    latent_grad = pl.pallas_call(
        functools.partial(finish_kernel, frames=frames, tile=tile),
        grid_spec=pltpu.PrefetchScalarGridSpec(
            num_scalar_prefetch=1,
            grid=(steps,),
            in_specs=[
                flat(own),
                pl.BlockSpec((2, own, cols), lambda g, *_: (0, 0, g)),
                side, side,
                pl.BlockSpec((count, 2, tile, cols), lambda g, *_: (0, 0, 0, g)),
                weight, weight, weight,
            ],
            out_specs=pl.BlockSpec((own, width), lambda g, *_: (0, 0)),
            scratch_shapes=[
                pltpu.VMEM((2, own, cols), jnp.float32),
                pltpu.VMEM((own, width), jnp.float32),
            ],
        ),
        out_shape=jax.ShapeDtypeStruct((own, width), jnp.bfloat16),
        compiler_params=pltpu.CompilerParams(vmem_limit_bytes=40 * 2**20),
    )(asked, query_grad, sums, from_below, from_above, back, w_query, w_key, w_value)
    return (layer_out, latent_grad.reshape(frames, tile, width))


def solution(mesh):
    placed = (
        P(("shard", "tm"), None, None),
        P(),
        P(),
        P(),
        P(),
        P(("shard", "tm"), None, None),
        P(("shard", "tm"), None),
        P(("shard", "tm")),
        P(("shard", "tm"), None),
    )
    return jax.shard_map(
        on_device,
        mesh=mesh,
        in_specs=placed,
        out_specs=(P(("shard", "tm"), None, None), P(("shard", "tm"), None, None)),
        check_vma=False,
    )
```

```python
import functools
import math

import jax
import jax.numpy as jnp
from jax import lax
from jax.experimental import pallas as pl
from jax.experimental.pallas import tpu as pltpu
from jax.sharding import PartitionSpec as P

HEADS = 24
GROUP = 4
NT = (((1,), (1,)), ((), ()))
NN = (((1,), (0,)), ((), ()))
TN = (((0,), (0,)), ((), ()))
MESH = pl.DeviceIdType.MESH


def dot(a, b, dims):
    return lax.dot_general(a, b, dims, preferred_element_type=jnp.float32)


def attend_kernel(
    count, frames, mem, tile, head_dim, steps,
    owners, place, valid, pick, q_ref, g_ref, k_ext, v_ext, k_mem, v_mem,
    wo_hbm, wq_hbm, wk_hbm, wv_hbm,
    layer_ref, grad_ref,
    weights, mixed, query_grad, sums, blocks, outgoing, incoming, total,
    weight_sem, send_sem, recv_sem, edge_send, edge_recv,
):
    me = lax.axis_index("tm")
    width = q_ref.shape[1]
    cols = width // steps
    rows = GROUP * tile
    inv_root = 1.0 / math.sqrt(head_dim)
    loads = [
        pltpu.make_async_copy(source, weights.at[i], weight_sem.at[i])
        for i, source in enumerate((wo_hbm, wq_hbm, wk_hbm, wv_hbm))
    ]
    for load in loads:
        load.start()

    barrier = pltpu.get_barrier_semaphore()

    @pl.loop(1, count)
    def _(d):
        pl.semaphore_signal(
            barrier, inc=1, device_id={"tm": lax.rem(me + d, count)}, device_id_type=MESH
        )

    own_head = (
        lax.broadcasted_iota(jnp.int32, (rows, cols), 0) // tile
        == lax.broadcasted_iota(jnp.int32, (rows, cols), 1) // head_dim
    )

    def spread(block):
        tall = jnp.concatenate([block] * GROUP, axis=0)
        return jnp.where(own_head, tall, jnp.zeros_like(tall))

    def fold(tall):
        tall = jnp.where(own_head, tall, 0.0)
        flat = tall[0:tile]
        for part in range(1, GROUP):
            flat = flat + tall[part * tile : (part + 1) * tile]
        return flat

    def push(g, d):
        return pltpu.make_async_remote_copy(
            src_ref=outgoing.at[g, d],
            dst_ref=incoming.at[g, d],
            send_sem=send_sem.at[g],
            recv_sem=recv_sem.at[g],
            device_id={"tm": lax.rem(me + d, count)},
            device_id_type=MESH,
        )

    def push_edge(g, side):
        return pltpu.make_async_remote_copy(
            src_ref=outgoing.at[g, count + side],
            dst_ref=incoming.at[g, count + side],
            send_sem=edge_send.at[g, side],
            recv_sem=edge_recv.at[g, side],
            device_id={"tm": lax.rem(me + (1 if side == 0 else count - 1), count)},
            device_id_type=MESH,
        )

    def attend(g):
        lanes = pl.ds(pl.multiple_of(g * cols, cols), cols)
        for f in range(frames):
            here = slice(f * tile, (f + 1) * tile)
            near = slice(f * tile, (f + 3) * tile)

            def gather(ext, far):
                return jnp.concatenate(
                    [ext[near, lanes]] + [far[owners[f * mem + j], :, lanes] for j in range(mem)],
                    axis=0,
                )

            keys = gather(k_ext, k_mem)
            values = gather(v_ext, v_mem)
            queries = spread(q_ref[here, lanes])
            grads = spread(g_ref[here, lanes])
            scores = dot(queries, keys, NT) * inv_root
            scores = jnp.where(valid[f : f + 1, :] > 0.5, scores, -1e30)
            expo = jnp.exp(scores - jnp.max(scores, axis=-1, keepdims=True))
            prob = expo / jnp.sum(expo, axis=-1, keepdims=True)
            low = prob.astype(jnp.bfloat16)
            mixed[here, lanes] = fold(dot(low, values, NN)).astype(jnp.bfloat16)
            prob_grad = dot(grads, values, NT)
            delta = jnp.sum(prob * prob_grad, axis=-1, keepdims=True)
            score_grad = (prob * (prob_grad - delta) * inv_root).astype(jnp.bfloat16)
            query_grad[here, lanes] = fold(dot(score_grad, keys, NN)).astype(jnp.bfloat16)
            parts = (
                dot(score_grad, queries, TN).astype(jnp.bfloat16),
                dot(low, grads, TN).astype(jnp.bfloat16),
            )
            for kv, part in enumerate(parts):
                before = part[0:tile]
                own = part[tile : 2 * tile].astype(jnp.float32)
                after = part[2 * tile : 3 * tile]
                if f == 0:
                    outgoing[g, count + 1, kv] = before
                    sums[kv, here, lanes] = own
                else:
                    back = slice((f - 1) * tile, f * tile)
                    sums[kv, back, lanes] += before.astype(jnp.float32)
                    sums[kv, here, lanes] += own
                if f == frames - 1:
                    outgoing[g, count, kv] = after
                else:
                    ahead = slice((f + 1) * tile, (f + 2) * tile)
                    sums[kv, ahead, lanes] = after.astype(jnp.float32)
                for j in range(mem):
                    blocks[f * mem + j, kv] = part[(3 + j) * tile : (4 + j) * tile]

    def send(g):
        @pl.loop(1, count)
        def _(d):
            outgoing[g, d] = blocks[place[lax.rem(me + d, count)]]
            push(g, d).start()

        push_edge(g, 0).start()
        push_edge(g, 1).start()
        incoming[g, 0] = blocks[place[me]]

    attend(0)
    pl.semaphore_wait(barrier, count - 1)
    send(0)

    @pl.loop(1, steps)
    def _(g):
        attend(g)
        send(g)

    for load in loads:
        load.wait()
    layer_ref[...] = dot(mixed[...], weights[0], NN).astype(jnp.bfloat16)
    total[...] = dot(query_grad[...], weights[1], NT)

    @pl.loop(0, steps)
    def _(g):
        lanes = pl.ds(pl.multiple_of(g * cols, cols), cols)
        others = pl.ds(1, count - 1)
        pltpu.make_async_copy(incoming.at[g, others], incoming.at[g, others], recv_sem.at[g]).wait()
        push_edge(g, 0).wait_recv()
        push_edge(g, 1).wait_recv()
        for kv in range(2):
            came = incoming[g, :, kv].reshape((count + 2) * tile, cols)
            whole = sums[kv, :, lanes] + dot(pick[...], came, NN)
            total[...] += dot(whole.astype(jnp.bfloat16), weights[2 + kv, :, lanes], NT)

    grad_ref[...] = total[...].astype(jnp.bfloat16)

    @pl.loop(0, steps)
    def _(g):
        others = pl.ds(1, count - 1)
        pltpu.make_async_copy(outgoing.at[g, others], outgoing.at[g, others], send_sem.at[g]).wait()
        push_edge(g, 0).wait_send()
        push_edge(g, 1).wait_send()


def on_device(
    latents, w_query, w_key, w_value, w_out, cotangent, memory_ids, memory_count, tile_mask
):
    frames, tile, width = latents.shape
    count = lax.axis_size("tm")
    me = lax.axis_index("tm")
    rows = latents.reshape(-1, width)
    mem = memory_ids.shape[1]
    inner = w_query.shape[1]
    head_dim = inner // HEADS
    cols = GROUP * head_dim
    steps = inner // cols
    up = [(i, i + 1) for i in range(count - 1)]
    down = [(i + 1, i) for i in range(count - 1)]

    owners = (memory_ids // frames).reshape(-1).astype(jnp.int32)
    local = (memory_ids % frames).reshape(-1).astype(jnp.int32)
    peers = jnp.arange(count, dtype=jnp.int32)
    matched = owners[None, :] == peers[:, None]
    wanted = jnp.where(
        jnp.any(matched, axis=1), jnp.sum(jnp.where(matched, local[None, :], 0), axis=1), -1
    )
    asked = lax.all_to_all(wanted[:, None], "tm", split_axis=0, concat_axis=0, tiled=True)[:, 0]
    frame_ids = jnp.arange(frames, dtype=jnp.int32)
    selector = (asked[:, None] == frame_ids[None, :]).astype(jnp.bfloat16)
    outgoing = jnp.einsum(
        "nf,ftc->ntc", selector, latents, preferred_element_type=jnp.float32
    ).astype(jnp.bfloat16)
    received = lax.all_to_all(outgoing, "tm", split_axis=0, concat_axis=0, tiled=True)
    below_rows = lax.ppermute(latents[frames - 1], "tm", up)
    above_rows = lax.ppermute(latents[0], "tm", down)

    def project(block, weight):
        return jnp.dot(block, weight, preferred_element_type=jnp.float32).astype(jnp.bfloat16)

    ext_rows = jnp.concatenate([below_rows, rows, above_rows], axis=0)
    queries = project(rows, w_query)
    k_ext = project(ext_rows, w_key)
    v_ext = project(ext_rows, w_value)
    out_grad = lax.dot_general(
        cotangent.reshape(-1, width), w_out, NT, preferred_element_type=jnp.float32
    ).astype(jnp.bfloat16)
    far_rows = received.reshape(count * tile, width)
    k_mem = project(far_rows, w_key).reshape(count, tile, inner)
    v_mem = project(far_rows, w_value).reshape(count, tile, inner)

    global_ids = me * frames + frame_ids
    lower = (tile_mask[:, 0] * (global_ids >= 1)).astype(jnp.float32)
    upper = (tile_mask[:, 1] * (global_ids < frames * count - 1)).astype(jnp.float32)
    kept = (jnp.arange(mem, dtype=jnp.int32)[None, :] < memory_count[:, None]).astype(jnp.float32)
    valid = jnp.concatenate(
        [lower[:, None], jnp.ones((frames, 1), jnp.float32), upper[:, None], kept], axis=1
    )
    valid = jnp.repeat(valid, tile, axis=1)

    own = frames * tile
    place = jnp.sum(
        jnp.where(matched, jnp.arange(frames * mem, dtype=jnp.int32)[None, :], 0), axis=1
    ).astype(jnp.int32)
    senders = (me - peers) % count
    ends = jnp.array([0, frames - 1], jnp.int32)
    came_for = jnp.concatenate([jnp.take(asked, senders), ends])
    token = jnp.arange(tile, dtype=jnp.int32)
    target = (came_for[:, None] * tile + token[None, :]).reshape(-1)
    target = jnp.where(jnp.repeat(came_for, tile) >= 0, target, -1)
    pick = (jnp.arange(own, dtype=jnp.int32)[:, None] == target[None, :]).astype(jnp.bfloat16)

    vmem = pl.BlockSpec(memory_space=pltpu.VMEM)
    smem = pl.BlockSpec(memory_space=pltpu.SMEM)
    hbm = pl.BlockSpec(memory_space=pl.ANY)
    block = (2, tile, cols)
    layer_out, latent_grad = pl.pallas_call(
        functools.partial(attend_kernel, count, frames, mem, tile, head_dim, steps),
        in_specs=[smem, smem] + [vmem] * 8 + [hbm] * 4,
        out_specs=[vmem, vmem],
        out_shape=[
            jax.ShapeDtypeStruct((own, width), jnp.bfloat16),
            jax.ShapeDtypeStruct((own, width), jnp.bfloat16),
        ],
        scratch_shapes=[
            pltpu.VMEM((4, width, inner), jnp.bfloat16),
            pltpu.VMEM((own, inner), jnp.bfloat16),
            pltpu.VMEM((own, inner), jnp.bfloat16),
            pltpu.VMEM((2, own, inner), jnp.float32),
            pltpu.VMEM((frames * mem,) + block, jnp.bfloat16),
            pltpu.VMEM((steps, count + 2) + block, jnp.bfloat16),
            pltpu.VMEM((steps, count + 2) + block, jnp.bfloat16),
            pltpu.VMEM((own, width), jnp.float32),
            pltpu.SemaphoreType.DMA((4,)),
            pltpu.SemaphoreType.DMA((steps,)),
            pltpu.SemaphoreType.DMA((steps,)),
            pltpu.SemaphoreType.DMA((steps, 2)),
            pltpu.SemaphoreType.DMA((steps, 2)),
        ],
        compiler_params=pltpu.CompilerParams(
            collective_id=0, has_side_effects=True, vmem_limit_bytes=56 * 2**20
        ),
    )(
        owners, place, valid, pick, queries, out_grad, k_ext, v_ext, k_mem, v_mem,
        w_out, w_query, w_key, w_value,
    )
    return (
        layer_out.reshape(frames, tile, width),
        latent_grad.reshape(frames, tile, width),
    )


def solution(mesh):
    placed = (
        P(("shard", "tm"), None, None),
        P(),
        P(),
        P(),
        P(),
        P(("shard", "tm"), None, None),
        P(("shard", "tm"), None),
        P(("shard", "tm")),
        P(("shard", "tm"), None),
    )
    return jax.shard_map(
        on_device,
        mesh=mesh,
        in_specs=placed,
        out_specs=(P(("shard", "tm"), None, None), P(("shard", "tm"), None, None)),
        check_vma=False,
    )
```

```python
import functools
import math

import jax
import jax.numpy as jnp
from jax import lax
from jax.experimental import pallas as pl
from jax.experimental.pallas import tpu as pltpu
from jax.sharding import PartitionSpec as P

HEADS = 24
GROUP = 4
NT = (((1,), (1,)), ((), ()))
NN = (((1,), (0,)), ((), ()))
TN = (((0,), (0,)), ((), ()))
MESH = pl.DeviceIdType.MESH


def dot(a, b, dims):
    return lax.dot_general(a, b, dims, preferred_element_type=jnp.float32)


CHUNK = 8


def layer_kernel(
    count, frames, mem, tile, head_dim, steps,
    spots, place, valid, x_ref, cot_ref, want_out,
    wq_hbm, wo_hbm, wk_hbm, wv_hbm,
    layer_ref, grad_ref,
    weights, q_ref, g_ref, k_ext, v_ext, k_mem, v_mem, want_in, choose, rows_out, rows_in,
    mixed, query_grad, sums, blocks, outgoing, incoming, total,
    weight_sem, want_send, want_recv, row_send, row_recv, halo_send, halo_recv,
    send_sem, recv_sem, edge_send, edge_recv,
):
    me = lax.axis_index("tm")
    width = q_ref.shape[1]
    own = q_ref.shape[0]
    cols = width // steps
    wide = 2 * cols
    rows = GROUP * tile
    inv_root = 1.0 / math.sqrt(head_dim)
    loads = [
        pltpu.make_async_copy(source, weights.at[i], weight_sem.at[i])
        for i, source in enumerate((wq_hbm, wo_hbm, wk_hbm, wv_hbm))
    ]
    for load in loads:
        load.start()

    def shift(i):
        half = i // 2
        return count // 2 + (i % 2) * 2 * half - half

    def peer(i):
        return {"tm": lax.rem(me + shift(i), count)}

    def asker(i):
        return {"tm": lax.rem(me + count - shift(i), count)}

    def beside(side):
        return {"tm": lax.rem(me + (1 if side == 0 else count - 1), count)}

    barrier = pltpu.get_barrier_semaphore()

    @pl.loop(1, count)
    def _(i):
        pl.semaphore_signal(barrier, inc=1, device_id=peer(i), device_id_type=MESH)

    pl.semaphore_wait(barrier, count - 1)

    def ask(i):
        return pltpu.make_async_remote_copy(
            src_ref=want_out.at[i], dst_ref=want_in.at[i], send_sem=want_send,
            recv_sem=want_recv, device_id=peer(i), device_id_type=MESH,
        )

    def push_halo(side):
        return pltpu.make_async_remote_copy(
            src_ref=x_ref.at[pl.ds((frames - 1) * tile if side == 0 else 0, tile)],
            dst_ref=rows_in.at[count + side],
            send_sem=halo_send.at[side], recv_sem=halo_recv.at[side],
            device_id=beside(side), device_id_type=MESH,
        )

    def push_row(i, c):
        return pltpu.make_async_remote_copy(
            src_ref=rows_out.at[i], dst_ref=rows_in.at[i], send_sem=row_send,
            recv_sem=row_recv.at[c], device_id=asker(i), device_id_type=MESH,
        )

    @pl.loop(1, count)
    def _(i):
        ask(i).start()

    push_halo(0).start()
    push_halo(1).start()
    want_in[0] = want_out[0]
    others = pl.ds(1, count - 1)
    pltpu.make_async_copy(want_in.at[others], want_in.at[others], want_recv).wait()

    chunks = count // CHUNK
    shape = (CHUNK, tile, own)
    token = lax.broadcasted_iota(jnp.int32, shape, 1)
    lane = lax.broadcasted_iota(jnp.int32, shape, 2)

    def pick_rows(c):
        asked = want_in[pl.ds(c * CHUNK, CHUNK)][:, 0:1, :]
        hot = jnp.where(lane == asked * tile + token, 1.0, 0.0).astype(jnp.bfloat16)
        hot = hot.reshape(CHUNK * tile, own)
        choose[pl.ds(pl.multiple_of(c * (CHUNK * tile), CHUNK * tile), CHUNK * tile), :] = hot
        for part in range(width // wide):
            lanes = slice(part * wide, (part + 1) * wide)
            rows_out[pl.ds(c * CHUNK, CHUNK), :, lanes] = (
                dot(hot, x_ref[:, lanes], NN).astype(jnp.bfloat16).reshape(CHUNK, tile, wide)
            )

    pick_rows(0)

    @pl.loop(1, CHUNK)
    def _(i):
        push_row(i, 0).start()

    rows_in[0] = rows_out[0]

    @pl.loop(1, chunks)
    def _(c):
        pick_rows(c)

        @pl.loop(0, CHUNK)
        def _(i):
            push_row(c * CHUNK + i, c).start()

    edge_row = lax.broadcasted_iota(jnp.int32, (2 * tile, own), 0)
    edge_lane = lax.broadcasted_iota(jnp.int32, (2 * tile, own), 1)
    edge_spot = jnp.where(edge_row < tile, edge_row, edge_row + (frames - 2) * tile)
    choose[count * tile : (count + 2) * tile, :] = jnp.where(
        edge_lane == edge_spot, 1.0, 0.0
    ).astype(jnp.bfloat16)

    loads[0].wait()

    @pl.loop(0, width // wide)
    def _(p):
        lanes = pl.ds(pl.multiple_of(p * wide, wide), wide)
        q_ref[:, lanes] = dot(x_ref[...], weights[0, :, lanes], NN).astype(jnp.bfloat16)

    loads[1].wait()

    @pl.loop(0, width // wide)
    def _(p):
        lanes = pl.ds(pl.multiple_of(p * wide, wide), wide)
        g_ref[:, lanes] = dot(cot_ref[...], weights[1, lanes, :], NT).astype(jnp.bfloat16)

    push_halo(0).wait_recv()
    push_halo(1).wait_recv()
    loads[2].wait()
    loads[3].wait()

    @pl.loop(0, width // wide)
    def _(p):
        lanes = pl.ds(pl.multiple_of(p * wide, wide), wide)
        ext = jnp.concatenate([rows_in[count], x_ref[...], rows_in[count + 1]], axis=0)
        k_ext[:, lanes] = dot(ext, weights[2, :, lanes], NN).astype(jnp.bfloat16)
        v_ext[:, lanes] = dot(ext, weights[3, :, lanes], NN).astype(jnp.bfloat16)

    def project(c):
        some = pl.ds(c * CHUNK, CHUNK)

        @pl.loop(0, width // wide)
        def _(p):
            lanes = pl.ds(pl.multiple_of(p * wide, wide), wide)
            flat = rows_in[some].reshape(CHUNK * tile, width)
            for weight, far in ((2, k_mem), (3, v_mem)):
                far[some, :, lanes] = (
                    dot(flat, weights[weight, :, lanes], NN)
                    .astype(jnp.bfloat16)
                    .reshape(CHUNK, tile, wide)
                )

    first = pl.ds(1, CHUNK - 1)
    pltpu.make_async_copy(rows_in.at[first], rows_in.at[first], row_recv.at[0]).wait()
    project(0)

    @pl.loop(1, chunks)
    def _(c):
        some = pl.ds(c * CHUNK, CHUNK)
        pltpu.make_async_copy(rows_in.at[some], rows_in.at[some], row_recv.at[c]).wait()
        project(c)

    own_head = (
        lax.broadcasted_iota(jnp.int32, (rows, cols), 0) // tile
        == lax.broadcasted_iota(jnp.int32, (rows, cols), 1) // head_dim
    )

    def spread(block):
        tall = jnp.concatenate([block] * GROUP, axis=0)
        return jnp.where(own_head, tall, jnp.zeros_like(tall))

    def fold(tall):
        tall = jnp.where(own_head, tall, 0.0)
        flat = tall[0:tile]
        for part in range(1, GROUP):
            flat = flat + tall[part * tile : (part + 1) * tile]
        return flat

    def push(g, d):
        return pltpu.make_async_remote_copy(
            src_ref=outgoing.at[g, d],
            dst_ref=incoming.at[g, d],
            send_sem=send_sem.at[g],
            recv_sem=recv_sem.at[g],
            device_id=peer(d),
            device_id_type=MESH,
        )

    def push_edge(g, side):
        return pltpu.make_async_remote_copy(
            src_ref=outgoing.at[g, count + side],
            dst_ref=incoming.at[g, count + side],
            send_sem=edge_send.at[g, side],
            recv_sem=edge_recv.at[g, side],
            device_id=beside(side),
            device_id_type=MESH,
        )

    def attend(g):
        lanes = pl.ds(pl.multiple_of(g * cols, cols), cols)
        for f in range(frames):
            here = slice(f * tile, (f + 1) * tile)
            near = slice(f * tile, (f + 3) * tile)

            def gather(ext, far):
                return jnp.concatenate(
                    [ext[near, lanes]] + [far[spots[f * mem + j], :, lanes] for j in range(mem)],
                    axis=0,
                )

            keys = gather(k_ext, k_mem)
            values = gather(v_ext, v_mem)
            queries = spread(q_ref[here, lanes])
            grads = spread(g_ref[here, lanes])
            scores = dot(queries, keys, NT) * inv_root
            scores = jnp.where(valid[f : f + 1, :] > 0.5, scores, -1e30)
            expo = jnp.exp(scores - jnp.max(scores, axis=-1, keepdims=True))
            prob = expo / jnp.sum(expo, axis=-1, keepdims=True)
            low = prob.astype(jnp.bfloat16)
            mixed[here, lanes] = fold(dot(low, values, NN)).astype(jnp.bfloat16)
            prob_grad = dot(grads, values, NT)
            delta = jnp.sum(prob * prob_grad, axis=-1, keepdims=True)
            score_grad = (prob * (prob_grad - delta) * inv_root).astype(jnp.bfloat16)
            query_grad[here, lanes] = fold(dot(score_grad, keys, NN)).astype(jnp.bfloat16)
            parts = (
                dot(score_grad, queries, TN).astype(jnp.bfloat16),
                dot(low, grads, TN).astype(jnp.bfloat16),
            )
            for kv, part in enumerate(parts):
                before = part[0:tile]
                own = part[tile : 2 * tile].astype(jnp.float32)
                after = part[2 * tile : 3 * tile]
                if f == 0:
                    outgoing[g, count + 1, kv] = before
                    sums[kv, here, lanes] = own
                else:
                    back = slice((f - 1) * tile, f * tile)
                    sums[kv, back, lanes] += before.astype(jnp.float32)
                    sums[kv, here, lanes] += own
                if f == frames - 1:
                    outgoing[g, count, kv] = after
                else:
                    ahead = slice((f + 1) * tile, (f + 2) * tile)
                    sums[kv, ahead, lanes] = after.astype(jnp.float32)
                for j in range(mem):
                    blocks[f * mem + j, kv] = part[(3 + j) * tile : (4 + j) * tile]

    def send(g):
        @pl.loop(1, count)
        def _(d):
            outgoing[g, d] = blocks[place[d]]
            push(g, d).start()

        push_edge(g, 0).start()
        push_edge(g, 1).start()
        incoming[g, 0] = blocks[place[0]]

    @pl.loop(0, steps)
    def _(g):
        attend(g)
        send(g)

    for part in range(width // wide):
        lanes = slice(part * wide, (part + 1) * wide)
        layer_ref[:, lanes] = dot(mixed[...], weights[1, :, lanes], NN).astype(jnp.bfloat16)
        total[:, lanes] = dot(query_grad[...], weights[0, lanes, :], NT)

    @pl.loop(0, steps)
    def _(g):
        lanes = pl.ds(pl.multiple_of(g * cols, cols), cols)
        pltpu.make_async_copy(incoming.at[g, others], incoming.at[g, others], recv_sem.at[g]).wait()
        push_edge(g, 0).wait_recv()
        push_edge(g, 1).wait_recv()
        for kv in range(2):
            came = incoming[g, :, kv].reshape((count + 2) * tile, cols)
            whole = sums[kv, :, lanes] + dot(choose[...], came, TN)
            total[...] += dot(whole.astype(jnp.bfloat16), weights[2 + kv, :, lanes], NT)

    grad_ref[...] = total[...].astype(jnp.bfloat16)
    pltpu.make_async_copy(want_out.at[others], want_out.at[others], want_send).wait()
    pltpu.make_async_copy(rows_out.at[others], rows_out.at[others], row_send).wait()
    push_halo(0).wait_send()
    push_halo(1).wait_send()

    @pl.loop(0, steps)
    def _(g):
        pltpu.make_async_copy(outgoing.at[g, others], outgoing.at[g, others], send_sem.at[g]).wait()
        push_edge(g, 0).wait_send()
        push_edge(g, 1).wait_send()


def on_device(
    latents, w_query, w_key, w_value, w_out, cotangent, memory_ids, memory_count, tile_mask
):
    frames, tile, width = latents.shape
    count = lax.axis_size("tm")
    me = lax.axis_index("tm")
    rows = latents.reshape(-1, width)
    mem = memory_ids.shape[1]
    inner = w_query.shape[1]
    head_dim = inner // HEADS
    cols = GROUP * head_dim
    steps = inner // cols
    order = jnp.arange(count, dtype=jnp.int32)
    half = order // 2
    shift = jnp.where(order == 0, 0, count // 2 + jnp.where(order % 2 == 1, half, -half))
    targets = (me + shift) % count

    owners = (memory_ids // frames).reshape(1, -1).astype(jnp.int32)
    local = (memory_ids % frames).reshape(1, -1).astype(jnp.int32)
    entry = jnp.arange(frames * mem, dtype=jnp.int32)
    spots = jnp.sum(jnp.where(targets[:, None] == owners, order[:, None], 0), axis=0)
    spots = spots.astype(jnp.int32)
    matched = targets[:, None] == owners
    place = jnp.sum(jnp.where(matched, entry[None, :], 0), axis=1).astype(jnp.int32)
    wanted = jnp.sum(jnp.where(matched, local + 1, 0), axis=1).astype(jnp.int32) - 1
    own = frames * tile
    want_out = jnp.broadcast_to(
        jnp.where(wanted < 0, -frames, wanted)[:, None, None], (count, 8, own)
    )
    frame_ids = jnp.arange(frames, dtype=jnp.int32)

    global_ids = me * frames + frame_ids
    lower = (tile_mask[:, 0] * (global_ids >= 1)).astype(jnp.float32)
    upper = (tile_mask[:, 1] * (global_ids < frames * count - 1)).astype(jnp.float32)
    kept = (jnp.arange(mem, dtype=jnp.int32)[None, :] < memory_count[:, None]).astype(jnp.float32)
    valid = jnp.concatenate(
        [lower[:, None], jnp.ones((frames, 1), jnp.float32), upper[:, None], kept], axis=1
    )
    valid = jnp.repeat(valid, tile, axis=1)

    vmem = pl.BlockSpec(memory_space=pltpu.VMEM)
    smem = pl.BlockSpec(memory_space=pltpu.SMEM)
    hbm = pl.BlockSpec(memory_space=pl.ANY)
    block = (2, tile, cols)
    layer_out, latent_grad = pl.pallas_call(
        functools.partial(layer_kernel, count, frames, mem, tile, head_dim, steps),
        in_specs=[smem, smem] + [vmem] * 4 + [hbm] * 4,
        out_specs=[vmem, vmem],
        out_shape=[
            jax.ShapeDtypeStruct((own, width), jnp.bfloat16),
            jax.ShapeDtypeStruct((own, width), jnp.bfloat16),
        ],
        scratch_shapes=[
            pltpu.VMEM((4, width, inner), jnp.bfloat16),
            pltpu.VMEM((own, inner), jnp.bfloat16),
            pltpu.VMEM((own, inner), jnp.bfloat16),
            pltpu.VMEM((own + 2 * tile, inner), jnp.bfloat16),
            pltpu.VMEM((own + 2 * tile, inner), jnp.bfloat16),
            pltpu.VMEM((count, tile, inner), jnp.bfloat16),
            pltpu.VMEM((count, tile, inner), jnp.bfloat16),
            pltpu.VMEM((count, 8, own), jnp.int32),
            pltpu.VMEM(((count + 2) * tile, own), jnp.bfloat16),
            pltpu.VMEM((count, tile, width), jnp.bfloat16),
            pltpu.VMEM((count + 2, tile, width), jnp.bfloat16),
            pltpu.VMEM((own, inner), jnp.bfloat16),
            pltpu.VMEM((own, inner), jnp.bfloat16),
            pltpu.VMEM((2, own, inner), jnp.float32),
            pltpu.VMEM((frames * mem,) + block, jnp.bfloat16),
            pltpu.VMEM((steps, count + 2) + block, jnp.bfloat16),
            pltpu.VMEM((steps, count + 2) + block, jnp.bfloat16),
            pltpu.VMEM((own, width), jnp.float32),
            pltpu.SemaphoreType.DMA((4,)),
            pltpu.SemaphoreType.DMA,
            pltpu.SemaphoreType.DMA,
            pltpu.SemaphoreType.DMA,
            pltpu.SemaphoreType.DMA((count // CHUNK,)),
            pltpu.SemaphoreType.DMA((2,)),
            pltpu.SemaphoreType.DMA((2,)),
            pltpu.SemaphoreType.DMA((steps,)),
            pltpu.SemaphoreType.DMA((steps,)),
            pltpu.SemaphoreType.DMA((steps, 2)),
            pltpu.SemaphoreType.DMA((steps, 2)),
        ],
        compiler_params=pltpu.CompilerParams(
            collective_id=0, has_side_effects=True, vmem_limit_bytes=58 * 2**20
        ),
    )(
        spots, place, valid, rows, cotangent.reshape(-1, width), want_out,
        w_query, w_out, w_key, w_value,
    )
    return (
        layer_out.reshape(frames, tile, width),
        latent_grad.reshape(frames, tile, width),
    )


def solution(mesh):
    placed = (
        P(("shard", "tm"), None, None),
        P(),
        P(),
        P(),
        P(),
        P(("shard", "tm"), None, None),
        P(("shard", "tm"), None),
        P(("shard", "tm")),
        P(("shard", "tm"), None),
    )
    return jax.shard_map(
        on_device,
        mesh=mesh,
        in_specs=placed,
        out_specs=(P(("shard", "tm"), None, None), P(("shard", "tm"), None, None)),
        check_vma=False,
    )
```

```python
import functools
import math

import jax
import jax.numpy as jnp
from jax import lax
from jax.experimental import pallas as pl
from jax.experimental.pallas import tpu as pltpu
from jax.sharding import PartitionSpec as P

HEADS = 24
GROUP = 4
NT = (((1,), (1,)), ((), ()))
NN = (((1,), (0,)), ((), ()))
TN = (((0,), (0,)), ((), ()))
MESH = pl.DeviceIdType.MESH


def dot(a, b, dims):
    return lax.dot_general(a, b, dims, preferred_element_type=jnp.float32)


CHUNK = 8


def layer_kernel(
    count, frames, mem, tile, head_dim, steps,
    spots, place, wanted, recalled, tiles, x_ref, cot_ref,
    wq_hbm, wo_hbm, wk_hbm, wv_hbm,
    layer_ref, grad_ref,
    weights, q_ref, g_ref, k_ext, v_ext, k_mem, v_mem, want_out, want_in, choose, rows_out, rows_in,
    mixed, query_grad, sums, blocks, outgoing, incoming, total,
    weight_sem, want_send, want_recv, row_send, row_recv, halo_send, halo_recv,
    send_sem, recv_sem, edge_send, edge_recv,
):
    me = lax.axis_index("tm")
    width = q_ref.shape[1]
    own = q_ref.shape[0]
    cols = width // steps
    wide = 2 * cols
    rows = GROUP * tile
    inv_root = 1.0 / math.sqrt(head_dim)
    loads = [
        pltpu.make_async_copy(source, weights.at[i], weight_sem.at[i])
        for i, source in enumerate((wq_hbm, wo_hbm, wk_hbm, wv_hbm))
    ]
    for load in loads:
        load.start()

    def shift(i):
        half = i // 2
        return count // 2 + (i % 2) * 2 * half - half

    def peer(i):
        return {"tm": lax.rem(me + shift(i), count)}

    def asker(i):
        return {"tm": lax.rem(me + count - shift(i), count)}

    def beside(side):
        return {"tm": lax.rem(me + (1 if side == 0 else count - 1), count)}

    barrier = pltpu.get_barrier_semaphore()

    @pl.loop(1, count)
    def _(i):
        pl.semaphore_signal(barrier, inc=1, device_id=peer(i), device_id_type=MESH)

    @pl.loop(0, count)
    def _(i):
        want_out[i] = jnp.full((8, own), wanted[i], jnp.int32)

    pl.semaphore_wait(barrier, count - 1)

    def ask(i):
        return pltpu.make_async_remote_copy(
            src_ref=want_out.at[i], dst_ref=want_in.at[i], send_sem=want_send,
            recv_sem=want_recv, device_id=peer(i), device_id_type=MESH,
        )

    def push_halo(side):
        return pltpu.make_async_remote_copy(
            src_ref=x_ref.at[pl.ds((frames - 1) * tile if side == 0 else 0, tile)],
            dst_ref=rows_in.at[count + side],
            send_sem=halo_send.at[side], recv_sem=halo_recv.at[side],
            device_id=beside(side), device_id_type=MESH,
        )

    def push_row(i, c):
        return pltpu.make_async_remote_copy(
            src_ref=rows_out.at[i], dst_ref=rows_in.at[i], send_sem=row_send,
            recv_sem=row_recv.at[c], device_id=asker(i), device_id_type=MESH,
        )

    @pl.loop(1, count)
    def _(i):
        ask(i).start()

    push_halo(0).start()
    push_halo(1).start()
    want_in[0] = want_out[0]
    others = pl.ds(1, count - 1)
    pltpu.make_async_copy(want_in.at[others], want_in.at[others], want_recv).wait()

    chunks = count // CHUNK
    shape = (CHUNK, tile, own)
    token = lax.broadcasted_iota(jnp.int32, shape, 1)
    lane = lax.broadcasted_iota(jnp.int32, shape, 2)

    def pick_rows(c):
        asked = want_in[pl.ds(c * CHUNK, CHUNK)][:, 0:1, :]
        hot = jnp.where(lane == asked * tile + token, 1.0, 0.0).astype(jnp.bfloat16)
        hot = hot.reshape(CHUNK * tile, own)
        choose[pl.ds(pl.multiple_of(c * (CHUNK * tile), CHUNK * tile), CHUNK * tile), :] = hot
        for part in range(width // wide):
            lanes = slice(part * wide, (part + 1) * wide)
            rows_out[pl.ds(c * CHUNK, CHUNK), :, lanes] = (
                dot(hot, x_ref[:, lanes], NN).astype(jnp.bfloat16).reshape(CHUNK, tile, wide)
            )

    pick_rows(0)

    @pl.loop(1, CHUNK)
    def _(i):
        push_row(i, 0).start()

    rows_in[0] = rows_out[0]

    @pl.loop(1, chunks)
    def _(c):
        pick_rows(c)

        @pl.loop(0, CHUNK)
        def _(i):
            push_row(c * CHUNK + i, c).start()

    edge_row = lax.broadcasted_iota(jnp.int32, (2 * tile, own), 0)
    edge_lane = lax.broadcasted_iota(jnp.int32, (2 * tile, own), 1)
    edge_spot = jnp.where(edge_row < tile, edge_row, edge_row + (frames - 2) * tile)
    choose[count * tile : (count + 2) * tile, :] = jnp.where(
        edge_lane == edge_spot, 1.0, 0.0
    ).astype(jnp.bfloat16)

    loads[0].wait()

    @pl.loop(0, width // wide)
    def _(p):
        lanes = pl.ds(pl.multiple_of(p * wide, wide), wide)
        q_ref[:, lanes] = dot(x_ref[...], weights[0, :, lanes], NN).astype(jnp.bfloat16)

    loads[1].wait()

    @pl.loop(0, width // wide)
    def _(p):
        lanes = pl.ds(pl.multiple_of(p * wide, wide), wide)
        g_ref[:, lanes] = dot(cot_ref[...], weights[1, lanes, :], NT).astype(jnp.bfloat16)

    push_halo(0).wait_recv()
    push_halo(1).wait_recv()
    loads[2].wait()
    loads[3].wait()

    @pl.loop(0, width // wide)
    def _(p):
        lanes = pl.ds(pl.multiple_of(p * wide, wide), wide)
        ext = jnp.concatenate([rows_in[count], x_ref[...], rows_in[count + 1]], axis=0)
        k_ext[:, lanes] = dot(ext, weights[2, :, lanes], NN).astype(jnp.bfloat16)
        v_ext[:, lanes] = dot(ext, weights[3, :, lanes], NN).astype(jnp.bfloat16)

    def project(c):
        some = pl.ds(c * CHUNK, CHUNK)

        @pl.loop(0, width // wide)
        def _(p):
            lanes = pl.ds(pl.multiple_of(p * wide, wide), wide)
            flat = rows_in[some].reshape(CHUNK * tile, width)
            for weight, far in ((2, k_mem), (3, v_mem)):
                far[some, :, lanes] = (
                    dot(flat, weights[weight, :, lanes], NN)
                    .astype(jnp.bfloat16)
                    .reshape(CHUNK, tile, wide)
                )

    first = pl.ds(1, CHUNK - 1)
    pltpu.make_async_copy(rows_in.at[first], rows_in.at[first], row_recv.at[0]).wait()
    project(0)

    @pl.loop(1, chunks)
    def _(c):
        some = pl.ds(c * CHUNK, CHUNK)
        pltpu.make_async_copy(rows_in.at[some], rows_in.at[some], row_recv.at[c]).wait()
        project(c)

    own_head = (
        lax.broadcasted_iota(jnp.int32, (rows, cols), 0) // tile
        == lax.broadcasted_iota(jnp.int32, (rows, cols), 1) // head_dim
    )

    def spread(block):
        tall = jnp.concatenate([block] * GROUP, axis=0)
        return jnp.where(own_head, tall, jnp.zeros_like(tall))

    def fold(tall):
        tall = jnp.where(own_head, tall, 0.0)
        flat = tall[0:tile]
        for part in range(1, GROUP):
            flat = flat + tall[part * tile : (part + 1) * tile]
        return flat

    def push(g, d):
        return pltpu.make_async_remote_copy(
            src_ref=outgoing.at[g, d],
            dst_ref=incoming.at[g, d],
            send_sem=send_sem.at[g],
            recv_sem=recv_sem.at[g],
            device_id=peer(d),
            device_id_type=MESH,
        )

    def push_edge(g, side):
        return pltpu.make_async_remote_copy(
            src_ref=outgoing.at[g, count + side],
            dst_ref=incoming.at[g, count + side],
            send_sem=edge_send.at[g, side],
            recv_sem=edge_recv.at[g, side],
            device_id=beside(side),
            device_id_type=MESH,
        )

    block_of = lax.broadcasted_iota(jnp.int32, (1, (3 + mem) * tile), 1) // tile

    def valid(f):
        frame = me * frames + f
        lower = jnp.where(frame >= 1, tiles[f, 0], 0)
        upper = jnp.where(frame < frames * count - 1, tiles[f, 1], 0)
        near = jnp.where(block_of == 0, lower, jnp.where(block_of == 1, 1, upper))
        kept = jnp.where(block_of - 3 < recalled[f], 1, 0)
        return jnp.where(block_of < 3, near, kept) > 0

    def attend(g):
        lanes = pl.ds(pl.multiple_of(g * cols, cols), cols)
        for f in range(frames):
            here = slice(f * tile, (f + 1) * tile)
            near = slice(f * tile, (f + 3) * tile)

            def gather(ext, far):
                return jnp.concatenate(
                    [ext[near, lanes]] + [far[spots[f * mem + j], :, lanes] for j in range(mem)],
                    axis=0,
                )

            keys = gather(k_ext, k_mem)
            values = gather(v_ext, v_mem)
            queries = spread(q_ref[here, lanes])
            grads = spread(g_ref[here, lanes])
            scores = dot(queries, keys, NT) * inv_root
            scores = jnp.where(valid(f), scores, -1e30)
            expo = jnp.exp(scores - jnp.max(scores, axis=-1, keepdims=True))
            prob = expo / jnp.sum(expo, axis=-1, keepdims=True)
            low = prob.astype(jnp.bfloat16)
            mixed[here, lanes] = fold(dot(low, values, NN)).astype(jnp.bfloat16)
            prob_grad = dot(grads, values, NT)
            delta = jnp.sum(prob * prob_grad, axis=-1, keepdims=True)
            score_grad = (prob * (prob_grad - delta) * inv_root).astype(jnp.bfloat16)
            query_grad[here, lanes] = fold(dot(score_grad, keys, NN)).astype(jnp.bfloat16)
            parts = (
                dot(score_grad, queries, TN).astype(jnp.bfloat16),
                dot(low, grads, TN).astype(jnp.bfloat16),
            )
            for kv, part in enumerate(parts):
                before = part[0:tile]
                own = part[tile : 2 * tile].astype(jnp.float32)
                after = part[2 * tile : 3 * tile]
                if f == 0:
                    outgoing[g, count + 1, kv] = before
                    sums[kv, here, lanes] = own
                else:
                    back = slice((f - 1) * tile, f * tile)
                    sums[kv, back, lanes] += before.astype(jnp.float32)
                    sums[kv, here, lanes] += own
                if f == frames - 1:
                    outgoing[g, count, kv] = after
                else:
                    ahead = slice((f + 1) * tile, (f + 2) * tile)
                    sums[kv, ahead, lanes] = after.astype(jnp.float32)
                for j in range(mem):
                    blocks[f * mem + j, kv] = part[(3 + j) * tile : (4 + j) * tile]

    def send(g):
        @pl.loop(1, count)
        def _(d):
            outgoing[g, d] = blocks[place[d]]
            push(g, d).start()

        push_edge(g, 0).start()
        push_edge(g, 1).start()
        incoming[g, 0] = blocks[place[0]]

    @pl.loop(0, steps)
    def _(g):
        attend(g)
        send(g)

    for part in range(width // wide):
        lanes = slice(part * wide, (part + 1) * wide)
        layer_ref[:, lanes] = dot(mixed[...], weights[1, :, lanes], NN).astype(jnp.bfloat16)
        total[:, lanes] = dot(query_grad[...], weights[0, lanes, :], NT)

    @pl.loop(0, steps)
    def _(g):
        lanes = pl.ds(pl.multiple_of(g * cols, cols), cols)
        pltpu.make_async_copy(incoming.at[g, others], incoming.at[g, others], recv_sem.at[g]).wait()
        push_edge(g, 0).wait_recv()
        push_edge(g, 1).wait_recv()
        for kv in range(2):
            came = incoming[g, :, kv].reshape((count + 2) * tile, cols)
            whole = sums[kv, :, lanes] + dot(choose[...], came, TN)
            total[...] += dot(whole.astype(jnp.bfloat16), weights[2 + kv, :, lanes], NT)

    grad_ref[...] = total[...].astype(jnp.bfloat16)
    pltpu.make_async_copy(want_out.at[others], want_out.at[others], want_send).wait()
    pltpu.make_async_copy(rows_out.at[others], rows_out.at[others], row_send).wait()
    push_halo(0).wait_send()
    push_halo(1).wait_send()

    @pl.loop(0, steps)
    def _(g):
        pltpu.make_async_copy(outgoing.at[g, others], outgoing.at[g, others], send_sem.at[g]).wait()
        push_edge(g, 0).wait_send()
        push_edge(g, 1).wait_send()


def on_device(
    latents, w_query, w_key, w_value, w_out, cotangent, memory_ids, memory_count, tile_mask
):
    frames, tile, width = latents.shape
    count = lax.axis_size("tm")
    me = lax.axis_index("tm")
    rows = latents.reshape(-1, width)
    mem = memory_ids.shape[1]
    inner = w_query.shape[1]
    head_dim = inner // HEADS
    cols = GROUP * head_dim
    steps = inner // cols
    order = jnp.arange(count, dtype=jnp.int32)
    half = order // 2
    shift = jnp.where(order == 0, 0, count // 2 + jnp.where(order % 2 == 1, half, -half))
    targets = (me + shift) % count

    owners = (memory_ids // frames).reshape(1, -1).astype(jnp.int32)
    local = (memory_ids % frames).reshape(1, -1).astype(jnp.int32)
    entry = jnp.arange(frames * mem, dtype=jnp.int32)
    spots = jnp.sum(jnp.where(targets[:, None] == owners, order[:, None], 0), axis=0)
    spots = spots.astype(jnp.int32)
    matched = targets[:, None] == owners
    place = jnp.sum(jnp.where(matched, entry[None, :], 0), axis=1).astype(jnp.int32)
    wanted = jnp.sum(jnp.where(matched, local + 1, 0), axis=1).astype(jnp.int32) - 1
    own = frames * tile
    wanted = jnp.where(wanted < 0, -frames, wanted)

    vmem = pl.BlockSpec(memory_space=pltpu.VMEM)
    smem = pl.BlockSpec(memory_space=pltpu.SMEM)
    hbm = pl.BlockSpec(memory_space=pl.ANY)
    block = (2, tile, cols)
    layer_out, latent_grad = pl.pallas_call(
        functools.partial(layer_kernel, count, frames, mem, tile, head_dim, steps),
        in_specs=[smem] * 5 + [vmem] * 2 + [hbm] * 4,
        out_specs=[vmem, vmem],
        out_shape=[
            jax.ShapeDtypeStruct((own, width), jnp.bfloat16),
            jax.ShapeDtypeStruct((own, width), jnp.bfloat16),
        ],
        scratch_shapes=[
            pltpu.VMEM((4, width, inner), jnp.bfloat16),
            pltpu.VMEM((own, inner), jnp.bfloat16),
            pltpu.VMEM((own, inner), jnp.bfloat16),
            pltpu.VMEM((own + 2 * tile, inner), jnp.bfloat16),
            pltpu.VMEM((own + 2 * tile, inner), jnp.bfloat16),
            pltpu.VMEM((count, tile, inner), jnp.bfloat16),
            pltpu.VMEM((count, tile, inner), jnp.bfloat16),
            pltpu.VMEM((count, 8, own), jnp.int32),
            pltpu.VMEM((count, 8, own), jnp.int32),
            pltpu.VMEM(((count + 2) * tile, own), jnp.bfloat16),
            pltpu.VMEM((count, tile, width), jnp.bfloat16),
            pltpu.VMEM((count + 2, tile, width), jnp.bfloat16),
            pltpu.VMEM((own, inner), jnp.bfloat16),
            pltpu.VMEM((own, inner), jnp.bfloat16),
            pltpu.VMEM((2, own, inner), jnp.float32),
            pltpu.VMEM((frames * mem,) + block, jnp.bfloat16),
            pltpu.VMEM((steps, count + 2) + block, jnp.bfloat16),
            pltpu.VMEM((steps, count + 2) + block, jnp.bfloat16),
            pltpu.VMEM((own, width), jnp.float32),
            pltpu.SemaphoreType.DMA((4,)),
            pltpu.SemaphoreType.DMA,
            pltpu.SemaphoreType.DMA,
            pltpu.SemaphoreType.DMA,
            pltpu.SemaphoreType.DMA((count // CHUNK,)),
            pltpu.SemaphoreType.DMA((2,)),
            pltpu.SemaphoreType.DMA((2,)),
            pltpu.SemaphoreType.DMA((steps,)),
            pltpu.SemaphoreType.DMA((steps,)),
            pltpu.SemaphoreType.DMA((steps, 2)),
            pltpu.SemaphoreType.DMA((steps, 2)),
        ],
        compiler_params=pltpu.CompilerParams(
            collective_id=0, has_side_effects=True, vmem_limit_bytes=58 * 2**20
        ),
    )(
        spots, place, wanted, memory_count, tile_mask, rows, cotangent.reshape(-1, width),
        w_query, w_out, w_key, w_value,
    )
    return (
        layer_out.reshape(frames, tile, width),
        latent_grad.reshape(frames, tile, width),
    )


def solution(mesh):
    placed = (
        P(("shard", "tm"), None, None),
        P(),
        P(),
        P(),
        P(),
        P(("shard", "tm"), None, None),
        P(("shard", "tm"), None),
        P(("shard", "tm")),
        P(("shard", "tm"), None),
    )
    return jax.shard_map(
        on_device,
        mesh=mesh,
        in_specs=placed,
        out_specs=(P(("shard", "tm"), None, None), P(("shard", "tm"), None, None)),
        check_vma=False,
    )
```
